32 devices in a mesh: shot: 8 (over z, core), brick: 4 (over y, x).
Axes of the slice: x: 2, y: 2, z: 4, core: 2. Of those that a mesh axis runs over, the one named last changes fastest.
Arguments:
- sources: float32 [8, 2, 2, 256, 32, 256], P('shot', None, None, None, 'brick'), may hold values from -24 to 24
- slowness: float32 [8, 256, 32, 256], P('shot', None, 'brick'), may hold values from 0.5 to 2
- group_size: int32 [8], replicated, may hold values from 2 to 4, as said below
- window_anchor: int32 [8], replicated, may hold values from 0 to 24
- tile_slot: int32 [32], replicated, may hold values from 0 to 31, each once
Outputs:
- gradient: float32 [4, 32, 65536], P('brick', 'shot')
The draws below stay inside these ranges and needn't reach their ends.
Inputs may be any that keep to these rules, and one draw needn't show every extreme that they name: `group_size`: some shot spans all 4 bricks and some shot only 2. Window s covers model tiles window_anchor[s] to window_anchor[s] + 7. `tile_slot`: each slot of 0 to 31 once.
All inputs are finite; a program needn't handle non-finite values.
Results may differ from the reference program's by a relative error of at most 0.0003.
Values sent between devices are 32-bit elements; how exact they have to be, the bound alone decides.
A program may use at most 128 MiB of HBM per device.

```python
import math
import jax
import jax.numpy as jnp
from jax import lax

PLANES = 8
WIDE_Y = 256
WIDE_Z = 256
BLOCKS = 8
SWEEPS = 2
SHOTS = 8
BANDS = 4
DEPTH = 32
TILES = 32
TILE_CELLS = 65536


def draw_group_size(key, part):
    shot_order = jax.random.permutation(jax.random.fold_in(key, 11), SHOTS)
    bricks_used = jax.random.randint(jax.random.fold_in(key, 12), (SHOTS,), 2, BANDS + 1, dtype=jnp.int32)
    bricks_used = bricks_used.at[shot_order[0]].set(BANDS)
    return bricks_used.at[shot_order[1]].set(2)


def touch_ends(entries, key, smallest, high):
    shape = entries.shape
    spot = [jax.random.randint(jax.random.fold_in(key, axis), (), 0, shape[axis]) for axis in range(len(shape))]
    entries = entries.at[tuple(spot)].set(smallest)
    longest = shape.index(max(shape))
    spot[longest] = (spot[longest] + 1) % shape[longest]
    return entries.at[tuple(spot)].set(high)


def steps_of(key, dims, shards, smallest, high):
    gain, own = 1.0, jax.random.fold_in(key, 6)
    for dim, parts in shards:
        heights = jnp.exp(jax.random.uniform(jax.random.fold_in(own, dim), (parts,), jnp.float32, smallest / len(shards), high / len(shards)))
        gain = gain * jnp.repeat(heights, dims[dim] // parts).reshape([-1 if axis == dim else 1 for axis in range(len(dims))])
    return gain


def normal_values(stream_key, shape, deviation, most, split=(), held_as=jnp.bfloat16):
    drawn = deviation * jax.random.normal(stream_key, shape, jnp.float32)
    if split:
        drawn = drawn * steps_of(stream_key, shape, split, -0.22, 0.18)
    return jnp.clip(drawn, -most, most).astype(held_as)


def setup_inputs(seed: int = 0) -> dict:
    splits = jax.random.split(jax.random.key(seed), 6)
    return {
        "sources": normal_values(splits[0], (SHOTS, 2, 2, WIDE_Y, DEPTH, WIDE_Z), 4.0, 24.0, ((0, 8), (4, 4)), jnp.float32),
        "slowness": jnp.clip(jnp.exp(math.log(2.0) - 1.3862944 * jax.random.uniform(splits[1], (SHOTS, WIDE_Y, DEPTH, WIDE_Z), jnp.float32) ** steps_of(splits[1], (SHOTS, WIDE_Y, DEPTH, WIDE_Z), ((0, 8), (2, 4)), -0.2, 0.2)), 0.5, 2.0),
        "group_size": draw_group_size(jax.random.fold_in(splits[5], 71), 0),
        "window_anchor": touch_ends(jax.random.randint(splits[3], (SHOTS,), 0, TILES - BLOCKS + 1), jax.random.fold_in(splits[3], 1), 0, TILES - BLOCKS).astype(jnp.int32),
        "tile_slot": jax.random.permutation(splits[4], TILES).astype(jnp.int32),
    }


shift_beta = 0.5
relaxation = 0.8


def neighbour_sum(field):
    summed = jnp.zeros_like(field)
    for along_axis in (1, 2, 3):
        widths = [(0, 0)] * 4
        widths[along_axis] = (1, 1)
        padded = jnp.pad(field, widths)
        count = field.shape[along_axis]
        summed = summed + lax.slice_in_dim(padded, 0, count, axis=along_axis)
        summed = summed + lax.slice_in_dim(padded, 2, count + 2, axis=along_axis)
    return summed


def apply_inverse(values, inv_re, inv_im):
    fwd_re = values[0] * inv_re - values[1] * inv_im
    fwd_im = values[0] * inv_im + values[1] * inv_re
    adj_re = values[2] * inv_re - values[3] * inv_im
    adj_im = values[2] * inv_im + values[3] * inv_re
    return jnp.stack([fwd_re, fwd_im, adj_re, adj_im])


def sine_taper(count, extent):
    positions = jnp.arange(count, dtype=jnp.int32).astype(jnp.float32)
    return jnp.sin(jnp.pi * (positions + 0.5) / extent)


def window_gradient(source_window, slowness_window, group_bricks):
    wide_y, depth, wide_z = slowness_window.shape
    extent = group_bricks * PLANES
    depth_ids = jnp.arange(depth, dtype=jnp.int32)
    active = depth_ids < extent
    active_mask = active.astype(jnp.float32)[None, :, None]
    real_d = 6.0 - slowness_window
    imag_d = shift_beta * slowness_window
    denominator = real_d * real_d + imag_d * imag_d
    inv_re = real_d / denominator
    inv_im = imag_d / denominator
    forcing = source_window.reshape(4, wide_y, depth, wide_z)
    field = jnp.zeros_like(forcing)
    for sweep_index in range(SWEEPS):
        updated = apply_inverse(forcing + neighbour_sum(field), inv_re, inv_im)
        field = ((1.0 - relaxation) * field + relaxation * updated) * active_mask
    imaging = field[0] * field[2] - field[1] * field[3] - shift_beta * (field[0] * field[3] + field[1] * field[2])
    extent_float = extent.astype(jnp.float32)
    depth_float = depth_ids.astype(jnp.float32)
    taper_x = jnp.where(active, jnp.sin(jnp.pi * (depth_float + 0.5) / extent_float), 0.0)
    taper_y = sine_taper(wide_y, float(wide_y))
    taper_z = sine_taper(wide_z, float(wide_z))
    gradient = imaging * (taper_y[:, None, None] * taper_x[None, :, None] * taper_z[None, None, :])
    banded = gradient.reshape(wide_y, BANDS, PLANES, wide_z).transpose(1, 0, 2, 3)
    return banded.reshape(BANDS, BLOCKS, TILE_CELLS)


def reference(sources, slowness, group_size, window_anchor, tile_slot):
    def one_shot(totals, shot_items):
        source_window, slowness_window, group_bricks, anchor = shot_items
        blocks = window_gradient(source_window, slowness_window, group_bricks)
        tile_slots = tile_slot[anchor + jnp.arange(BLOCKS, dtype=jnp.int32)]
        totals = totals.at[:, tile_slots, :].add(blocks)
        return totals, None

    start = jnp.zeros((BANDS, TILES, TILE_CELLS), jnp.float32)
    totals, unused = lax.scan(one_shot, start, (sources, slowness, group_size, window_anchor))
    return totals
```

```python
import functools

import jax
import jax.numpy as jnp
from jax import lax
from jax.experimental import pallas as pl
from jax.experimental.pallas import tpu as pltpu
from jax.sharding import PartitionSpec as P

BLOCKS = 8
ROWS = 2
MESH = pl.DeviceIdType.MESH

shift_beta = 0.5
relaxation = 0.8


def kernel(
    shots, bricks, per_dev, chunks,
    mask_ref, ty_ref, wt_ref, txz_ref, src_ref, slow_ref,
    out_ref,
    sbuf, wbuf, f1, inv, hs_up, hs_dn, h_before, h_after, gsend, raw,
    rin, rout, lin, lout, own, fin,
    in_sem, win_sem, up_s, up_r, dn_s, dn_r, sib_s, sib_r, rt_s, rt_r, lt_s, lt_r, fin_s, fin_r,
):
    shot = lax.axis_index("shot")
    brick = lax.axis_index("brick")
    pair, core = shot // 2, shot % 2
    sib = pair * 2 + (1 - core)
    pairs = shots // 2
    group = 2 * per_dev
    both = 2 * BLOCKS
    half_rows = chunks * ROWS
    wide_y = 2 * BLOCKS * half_rows

    def source_copies(k, slot):
        return (
            pltpu.make_async_copy(src_ref.at[:, :, k], sbuf.at[slot], in_sem.at[slot]),
            pltpu.make_async_copy(slow_ref.at[:, k], wbuf.at[slot], win_sem.at[slot]),
        )

    for copy in source_copies(0, 0):
        copy.start()

    barrier = pltpu.get_barrier_semaphore()

    def greet(s, b):
        pl.semaphore_signal(barrier, inc=1, device_id=(s, b), device_id_type=MESH)

    greet(sib, brick)

    @pl.when(brick > 0)
    def _():
        greet(shot, brick - 1)

    @pl.when(brick < bricks - 1)
    def _():
        greet(shot, brick + 1)

    @pl.when(pair > 0)
    def _():
        greet(shot - 2, brick)

    @pl.when(pair < pairs - 1)
    def _():
        greet(shot + 2, brick)

    @pl.when(brick == 0)
    def _():
        h_before[...] = jnp.zeros_like(h_before)

    @pl.when(brick == bricks - 1)
    def _():
        h_after[...] = jnp.zeros_like(h_after)

    zero_row = jnp.zeros((1,) + f1.shape[2:], jnp.float32)
    for c in range(4):
        f1[c, pl.ds(0, 1)] = zero_row
        f1[c, pl.ds(wide_y + 1, 1)] = zero_row

    one = jnp.int32(1)
    nothing = jnp.int32(0)
    friends = (
        one
        + jnp.where(brick > 0, one, nothing)
        + jnp.where(brick < bricks - 1, one, nothing)
        + jnp.where(pair > 0, one, nothing)
        + jnp.where(pair < pairs - 1, one, nothing)
    )
    pl.semaphore_wait(barrier, friends)

    def up_copy(k):
        return pltpu.make_async_remote_copy(
            src_ref=hs_up.at[k], dst_ref=h_before.at[k], send_sem=up_s.at[k], recv_sem=up_r.at[k],
            device_id=(shot, brick + 1), device_id_type=MESH)

    def dn_copy(k):
        return pltpu.make_async_remote_copy(
            src_ref=hs_dn.at[k], dst_ref=h_after.at[k], send_sem=dn_s.at[k], recv_sem=dn_r.at[k],
            device_id=(shot, brick - 1), device_id_type=MESH)

    mask = mask_ref[0]

    def first(k, carry):
        slot = lax.rem(k, 2)

        @pl.when(k + 1 < chunks)
        def _():
            for copy in source_copies(k + 1, 1 - slot):
                copy.start()

        for copy in source_copies(k, slot):
            copy.wait()

        def rows(j, carry):
            y = j * half_rows + k * ROWS
            w = wbuf[slot, j]
            real_d = 6.0 - w
            imag_d = shift_beta * w
            scale = relaxation / (real_d * real_d + imag_d * imag_d)
            ire = real_d * scale
            iim = imag_d * scale
            inv[0, pl.ds(y, ROWS)] = ire
            inv[1, pl.ds(y, ROWS)] = iim
            mre, mim = ire * mask, iim * mask
            for p in range(2):
                a, b = sbuf[slot, 2 * p, j], sbuf[slot, 2 * p + 1, j]
                fre = a * mre - b * mim
                fim = a * mim + b * mre
                for c, f in ((2 * p, fre), (2 * p + 1, fim)):
                    f1[c, pl.ds(y + 1, ROWS)] = f
                    for r in range(ROWS):
                        hs_dn[k, c, pl.ds(j * ROWS + r, 1), :] = f[r, 0:1, :]
                        hs_up[k, c, pl.ds(j * ROWS + r, 1), :] = f[r, 7:8, :]
            return carry

        lax.fori_loop(0, both, rows, 0)

        @pl.when(brick < bricks - 1)
        def _():
            up_copy(k).start()

        @pl.when(brick > 0)
        def _():
            dn_copy(k).start()

        return carry

    lax.fori_loop(0, chunks, first, 0)

    planes, wide_z = f1.shape[2:]
    lane = lax.broadcasted_iota(jnp.int32, (planes, wide_z), 1)
    sub = lax.broadcasted_iota(jnp.int32, (planes, wide_z), 0)

    def image(k, j, r):
        y = j * half_rows + k * ROWS + r
        hrow = j * ROWS + r
        centre, near = [], []
        for c in range(4):
            f = f1[c, y + 1]
            total = f1[c, y] + f1[c, y + 2]
            total += jnp.where(lane == 0, 0.0, pltpu.roll(f, 1, axis=1))
            total += jnp.where(lane == wide_z - 1, 0.0, pltpu.roll(f, wide_z - 1, axis=1))
            total += jnp.where(sub == 0, h_before[k, c, pl.ds(hrow, 1), :], pltpu.roll(f, 1, axis=0))
            total += jnp.where(sub == planes - 1, h_after[k, c, pl.ds(hrow, 1), :], pltpu.roll(f, planes - 1, axis=0))
            centre.append(f)
            near.append(total)
        ire, iim = inv[0, y], inv[1, y]
        keep = 2.0 - relaxation
        field = []
        for p in (0, 2):
            field.append(keep * centre[p] + (near[p] * ire - near[p + 1] * iim))
            field.append(keep * centre[p + 1] + (near[p] * iim + near[p + 1] * ire))
        imaging = (
            field[0] * field[2]
            - field[1] * field[3]
            - shift_beta * (field[0] * field[3] + field[1] * field[2])
        )
        return imaging * (txz_ref[...] * ty_ref[y])

    def sib_copy(k):
        return pltpu.make_async_remote_copy(
            src_ref=gsend.at[k], dst_ref=raw.at[k, pl.ds(core * BLOCKS, BLOCKS)],
            send_sem=sib_s.at[k], recv_sem=sib_r.at[k],
            device_id=(sib, brick), device_id_type=MESH)

    def sib_wait(k):
        pltpu.make_async_remote_copy(
            src_ref=gsend.at[k], dst_ref=raw.at[k, pl.ds((1 - core) * BLOCKS, BLOCKS)],
            send_sem=sib_s.at[k], recv_sem=sib_r.at[k],
            device_id=(sib, brick), device_id_type=MESH).wait_recv()

    def right_copy(k, s):
        count = both if s == 0 else (pairs - 1 - s) * group
        return pltpu.make_async_remote_copy(
            src_ref=raw.at[k] if s == 0 else rout.at[k, pl.ds(0, count)],
            dst_ref=rin.at[k, pl.ds(0, count)],
            send_sem=rt_s.at[k], recv_sem=rt_r.at[k],
            device_id=(2 * (s + 1) + core, brick), device_id_type=MESH)

    def left_copy(k, s):
        count = both if s == pairs - 1 else s * group
        return pltpu.make_async_remote_copy(
            src_ref=raw.at[k] if s == pairs - 1 else lout.at[k, pl.ds(0, count)],
            dst_ref=lin.at[k, pl.ds(0, count)],
            send_sem=lt_s.at[k], recv_sem=lt_r.at[k],
            device_id=(2 * (s - 1) + core, brick), device_id_type=MESH)

    def fin_copy(k):
        return pltpu.make_async_remote_copy(
            src_ref=own.at[k, pl.ds((1 - core) * per_dev, per_dev)], dst_ref=fin.at[k],
            send_sem=fin_s.at[k], recv_sem=fin_r.at[k],
            device_id=(sib, brick), device_id_type=MESH)

    def weighted(buf, k, r, source_pair):
        start = (r * shots + 2 * source_pair) * BLOCKS
        total = wt_ref[start] * buf[k, 0]
        for q in range(1, both):
            total += wt_ref[start + q] * buf[k, q]
        return total

    def produce(k):
        @pl.when(brick > 0)
        def _():
            pltpu.make_async_remote_copy(
                src_ref=hs_up.at[k], dst_ref=h_before.at[k], send_sem=up_s.at[k], recv_sem=up_r.at[k],
                device_id=(shot, brick - 1), device_id_type=MESH).wait_recv()

        @pl.when(brick < bricks - 1)
        def _():
            pltpu.make_async_remote_copy(
                src_ref=hs_dn.at[k], dst_ref=h_after.at[k], send_sem=dn_s.at[k], recv_sem=dn_r.at[k],
                device_id=(shot, brick + 1), device_id_type=MESH).wait_recv()

        def other(b, carry):
            for r in range(ROWS):
                gsend[k, b, r] = image(k, 2 * b + (1 - core), r)
            return carry

        lax.fori_loop(0, BLOCKS, other, 0)
        sib_copy(k).start()

        def mine(b, carry):
            for r in range(ROWS):
                raw[k, core * BLOCKS + b, r] = image(k, 2 * b + core, r)
            return carry

        lax.fori_loop(0, BLOCKS, mine, 0)

    def right_flow(k):
        for s in range(pairs - 1):
            @pl.when(pair == s + 1)
            def _(s=s):
                right_copy(k, s).wait_recv()

        for s in range(pairs - 1):
            @pl.when(pair == s)
            def _(s=s):
                if s > 0:
                    def body(q, carry):
                        r = (s + 1) * group + q
                        total = weighted(raw, k, r, s)
                        if s == 1:
                            total += weighted(rin, k, r, 0)
                        else:
                            total += rin[k, q + group]
                        rout[k, q] = total
                        return carry

                    lax.fori_loop(0, (pairs - 1 - s) * group, body, 0)
                right_copy(k, s).start()

    def left_flow(k):
        for s in range(1, pairs):
            @pl.when(pair == s - 1)
            def _(s=s):
                left_copy(k, s).wait_recv()

        for s in range(1, pairs):
            @pl.when(pair == s)
            def _(s=s):
                if s < pairs - 1:
                    def body(q, carry):
                        total = weighted(raw, k, q, s)
                        if s == pairs - 2:
                            total += weighted(lin, k, q, pairs - 1)
                        else:
                            total += lin[k, q]
                        lout[k, q] = total
                        return carry

                    lax.fori_loop(0, s * group, body, 0)
                left_copy(k, s).start()

    def finish(k):
        for s in range(pairs):
            @pl.when(pair == s)
            def _(s=s):
                def body(q, carry):
                    r = s * group + q
                    total = weighted(raw, k, r, s)
                    if s == 1:
                        total += weighted(rin, k, r, 0)
                    elif s > 1:
                        total += rin[k, q]
                    if s == pairs - 2:
                        total += weighted(lin, k, r, pairs - 1)
                    elif s < pairs - 1:
                        total += lin[k, s * group + q]
                    own[k, q] = total
                    return carry

                lax.fori_loop(0, group, body, 0)

        fin_copy(k).start()
        for q in range(per_dev):
            out_ref[q, core, k] = own[k, core * per_dev + q]

    near_lag, far_lag, end_lag = 1, 2, 3
    is_left = pair < pairs // 2
    right_lag = jnp.where(is_left, near_lag, far_lag)
    left_lag = jnp.where(is_left, far_lag, near_lag)

    def step(t, carry):
        @pl.when(t < chunks)
        def _():
            produce(t)

        @pl.when((t >= 1) & (t < chunks + 1))
        def _():
            sib_wait(t - 1)

        kr = t - right_lag
        kl = t - left_lag

        @pl.when((kr >= 0) & (kr < chunks))
        def _():
            right_flow(kr)

        @pl.when((kl >= 0) & (kl < chunks))
        def _():
            left_flow(kl)

        @pl.when(t >= end_lag)
        def _():
            finish(t - end_lag)

        return carry

    lax.fori_loop(0, chunks + end_lag, step, 0)

    def drain(k, carry):
        fin_copy(k).wait_recv()
        for q in range(per_dev):
            out_ref[q, 1 - core, k] = fin[k, q]
        fin_copy(k).wait_send()
        sib_copy(k).wait_send()

        @pl.when(brick < bricks - 1)
        def _():
            up_copy(k).wait_send()

        @pl.when(brick > 0)
        def _():
            dn_copy(k).wait_send()

        for s in range(pairs - 1):
            @pl.when(pair == s)
            def _(s=s):
                right_copy(k, s).wait_send()

            @pl.when(pair == s + 1)
            def _(s=s):
                left_copy(k, s + 1).wait_send()

        return carry

    lax.fori_loop(0, chunks, drain, 0)


def sine_taper(count, extent):
    positions = jnp.arange(count, dtype=jnp.int32).astype(jnp.float32)
    return jnp.sin(jnp.pi * (positions + 0.5) / extent)


def per_device(shots, bricks, sources, slowness, group_size, window_anchor, tile_slot):
    wide_y, planes, wide_z = slowness.shape[1:]
    half_rows = wide_y // (2 * BLOCKS)
    chunks = half_rows // ROWS
    brick_index = lax.axis_index("brick")
    shot_index = lax.axis_index("shot")
    tiles = tile_slot.shape[0]
    per_dev = tiles // shots
    pairs = shots // 2
    group = 2 * per_dev
    both = 2 * BLOCKS

    extent = group_size[shot_index] * planes
    depth_ids = brick_index * planes + jnp.arange(planes, dtype=jnp.int32)
    active = depth_ids < extent
    mask = (brick_index < group_size[shot_index]).astype(jnp.float32).reshape(1)
    taper_x = jnp.where(
        active,
        jnp.sin(jnp.pi * (depth_ids.astype(jnp.float32) + 0.5) / extent.astype(jnp.float32)),
        0.0,
    )
    taper_xz = taper_x[:, None] * sine_taper(wide_z, float(wide_z))[None, :]
    taper_y = sine_taper(wide_y, float(wide_y))
    piece_slots = tile_slot[window_anchor[:, None] + jnp.arange(BLOCKS, dtype=jnp.int32)[None, :]]
    slots = jnp.arange(tiles, dtype=jnp.int32)
    weights = (slots[:, None, None] == piece_slots[None]).astype(jnp.float32).reshape(-1)

    chunk = (ROWS, planes, wide_z)
    src = sources.reshape((4, 2 * BLOCKS, chunks) + chunk)
    slow = slowness.reshape((2 * BLOCKS, chunks) + chunk)
    f32 = jnp.float32
    wide = max(both, (pairs - 2) * group)
    fwd = max(group, (pairs - 2) * group)
    dma = pltpu.SemaphoreType.DMA
    smem = pl.BlockSpec(memory_space=pltpu.SMEM)
    vmem = pl.BlockSpec(memory_space=pltpu.VMEM)
    hbm = pl.BlockSpec(memory_space=pl.ANY)
    halo = pltpu.VMEM((chunks, 4, both * ROWS, wide_z), f32)
    out = pl.pallas_call(
        functools.partial(kernel, shots, bricks, per_dev, chunks),
        out_shape=jax.ShapeDtypeStruct((per_dev, 2, chunks) + chunk, f32),
        in_specs=[smem, smem, smem, vmem, hbm, hbm],
        out_specs=vmem,
        scratch_shapes=[
            pltpu.VMEM((2, 4, both) + chunk, f32),
            pltpu.VMEM((2, both) + chunk, f32),
            pltpu.VMEM((4, wide_y + 2, planes, wide_z), f32),
            pltpu.VMEM((2, wide_y, planes, wide_z), f32),
            halo, halo, halo, halo,
            pltpu.VMEM((chunks, BLOCKS) + chunk, f32),
            pltpu.VMEM((chunks, both) + chunk, f32),
            pltpu.VMEM((chunks, wide) + chunk, f32),
            pltpu.VMEM((chunks, fwd) + chunk, f32),
            pltpu.VMEM((chunks, wide) + chunk, f32),
            pltpu.VMEM((chunks, fwd) + chunk, f32),
            pltpu.VMEM((chunks, group) + chunk, f32),
            pltpu.VMEM((chunks, per_dev) + chunk, f32),
            dma((2,)), dma((2,)),
        ] + [dma((chunks,))] * 12,
        compiler_params=pltpu.CompilerParams(
            collective_id=0, has_side_effects=True, vmem_limit_bytes=62 * 1024 * 1024
        ),
        cost_estimate=pl.CostEstimate(
            flops=200 * wide_y * planes * wide_z, bytes_accessed=12 * 1024 * 1024, transcendentals=0
        ),
    )(mask, taper_y, weights, taper_xz, src, slow)
    return out.reshape(1, per_dev, -1)


def solution(mesh):
    return jax.shard_map(
        functools.partial(per_device, mesh.shape["shot"], mesh.shape["brick"]),
        mesh=mesh,
        in_specs=(
            P("shot", None, None, None, "brick", None),
            P("shot", None, "brick", None),
            P(),
            P(),
            P(),
        ),
        out_specs=P("brick", "shot", None),
        check_vma=False,
    )
```

```python
import functools

import jax
import jax.numpy as jnp
from jax import lax
from jax.experimental import pallas as pl
from jax.experimental.pallas import tpu as pltpu
from jax.sharding import PartitionSpec as P

BLOCKS = 8
WIDTH = 4
ROWS = 2
MESH = pl.DeviceIdType.MESH

shift_beta = 0.5
relaxation = 0.8


def kernel(
    shots, bricks, per_dev, chunks,
    mask_ref, ty_ref, wt_ref, txz_ref, src_ref, slow_ref,
    out_ref,
    sbuf, wbuf, f1, inv, hs_up, hs_dn, h_before, h_after, gsend, raw,
    rin, rout, lin, lout, own, fin,
    in_sem, win_sem, up_s, up_r, dn_s, dn_r, sib_s, sib_r, rt_s, rt_r, lt_s, lt_r, fin_s, fin_r,
):
    shot = lax.axis_index("shot")
    brick = lax.axis_index("brick")
    pair, core = shot // 2, shot % 2
    sib = pair * 2 + (1 - core)
    pairs = shots // 2
    group = 2 * per_dev
    both = 2 * BLOCKS
    half_rows = chunks * ROWS
    wide_y = 2 * BLOCKS * half_rows

    def source_copies(k, slot):
        return (
            pltpu.make_async_copy(src_ref.at[:, :, k], sbuf.at[slot], in_sem.at[slot]),
            pltpu.make_async_copy(slow_ref.at[:, k], wbuf.at[slot], win_sem.at[slot]),
        )

    for copy in source_copies(0, 0):
        copy.start()

    barrier = pltpu.get_barrier_semaphore()

    def greet(s, b):
        pl.semaphore_signal(barrier, inc=1, device_id=(s, b), device_id_type=MESH)

    greet(sib, brick)

    @pl.when(brick > 0)
    def _():
        greet(shot, brick - 1)

    @pl.when(brick < bricks - 1)
    def _():
        greet(shot, brick + 1)

    @pl.when(pair > 0)
    def _():
        greet(shot - 2, brick)

    @pl.when(pair < pairs - 1)
    def _():
        greet(shot + 2, brick)

    @pl.when(brick == 0)
    def _():
        h_before[...] = jnp.zeros_like(h_before)

    @pl.when(brick == bricks - 1)
    def _():
        h_after[...] = jnp.zeros_like(h_after)

    zero_row = jnp.zeros((1,) + f1.shape[2:], jnp.float32)
    for c in range(4):
        f1[c, pl.ds(0, 1)] = zero_row
        f1[c, pl.ds(wide_y + 1, 1)] = zero_row

    one = jnp.int32(1)
    nothing = jnp.int32(0)
    friends = (
        one
        + jnp.where(brick > 0, one, nothing)
        + jnp.where(brick < bricks - 1, one, nothing)
        + jnp.where(pair > 0, one, nothing)
        + jnp.where(pair < pairs - 1, one, nothing)
    )
    pl.semaphore_wait(barrier, friends)

    def up_copy(k):
        return pltpu.make_async_remote_copy(
            src_ref=hs_up.at[k], dst_ref=h_before.at[k], send_sem=up_s.at[k], recv_sem=up_r.at[k],
            device_id=(shot, brick + 1), device_id_type=MESH)

    def dn_copy(k):
        return pltpu.make_async_remote_copy(
            src_ref=hs_dn.at[k], dst_ref=h_after.at[k], send_sem=dn_s.at[k], recv_sem=dn_r.at[k],
            device_id=(shot, brick - 1), device_id_type=MESH)

    mask = mask_ref[0]

    def first(k, carry):
        slot = lax.rem(k, 2)

        @pl.when(k + 1 < chunks)
        def _():
            for copy in source_copies(k + 1, 1 - slot):
                copy.start()

        for copy in source_copies(k, slot):
            copy.wait()

        def rows(j, carry):
            y = j * half_rows + k * ROWS
            w = wbuf[slot, j]
            real_d = 6.0 - w
            imag_d = shift_beta * w
            scale = relaxation / (real_d * real_d + imag_d * imag_d)
            ire = real_d * scale
            iim = imag_d * scale
            inv[0, pl.ds(y, ROWS)] = ire
            inv[1, pl.ds(y, ROWS)] = iim
            mre, mim = ire * mask, iim * mask
            fields = []
            for p in range(2):
                a, b = sbuf[slot, 2 * p, j], sbuf[slot, 2 * p + 1, j]
                fields += [a * mre - b * mim, a * mim + b * mre]
            for c, f in enumerate(fields):
                f1[c, pl.ds(y + 1, ROWS)] = f
                for r in range(ROWS):
                    hs_dn[k, c, pl.ds(j * ROWS + r, 1), :] = f[r, 0:1, :]
                    hs_up[k, c, pl.ds(j * ROWS + r, 1), :] = f[r, 7:8, :]
            return carry

        lax.fori_loop(0, both, rows, 0)

        @pl.when(brick < bricks - 1)
        def _():
            up_copy(k).start()

        @pl.when(brick > 0)
        def _():
            dn_copy(k).start()

        return carry

    lax.fori_loop(0, chunks, first, 0)

    planes, wide_z = f1.shape[2:]
    lane = lax.broadcasted_iota(jnp.int32, (planes, wide_z), 1)
    sub = lax.broadcasted_iota(jnp.int32, (planes, wide_z), 0)

    def image(k, j, r):
        y = j * half_rows + k * ROWS + r
        hrow = j * ROWS + r
        centre, near = [], []
        for c in range(4):
            f = f1[c, y + 1]
            total = f1[c, y] + f1[c, y + 2]
            total += jnp.where(lane == 0, 0.0, pltpu.roll(f, 1, axis=1))
            total += jnp.where(lane == wide_z - 1, 0.0, pltpu.roll(f, wide_z - 1, axis=1))
            total += jnp.where(sub == 0, h_before[k, c, pl.ds(hrow, 1), :], pltpu.roll(f, 1, axis=0))
            total += jnp.where(sub == planes - 1, h_after[k, c, pl.ds(hrow, 1), :], pltpu.roll(f, planes - 1, axis=0))
            centre.append(f)
            near.append(total)
        ire, iim = inv[0, y], inv[1, y]
        keep = 2.0 - relaxation
        field = []
        for p in (0, 2):
            field.append(keep * centre[p] + (near[p] * ire - near[p + 1] * iim))
            field.append(keep * centre[p + 1] + (near[p] * iim + near[p + 1] * ire))
        imaging = (
            field[0] * field[2]
            - field[1] * field[3]
            - shift_beta * (field[0] * field[3] + field[1] * field[2])
        )
        return imaging * (txz_ref[...] * ty_ref[y])

    def sib_copy(k):
        return pltpu.make_async_remote_copy(
            src_ref=gsend.at[k], dst_ref=raw.at[k, pl.ds(core * BLOCKS, BLOCKS)],
            send_sem=sib_s.at[k], recv_sem=sib_r.at[k],
            device_id=(sib, brick), device_id_type=MESH)

    def sib_wait(k):
        pltpu.make_async_remote_copy(
            src_ref=gsend.at[k], dst_ref=raw.at[k, pl.ds((1 - core) * BLOCKS, BLOCKS)],
            send_sem=sib_s.at[k], recv_sem=sib_r.at[k],
            device_id=(sib, brick), device_id_type=MESH).wait_recv()

    def right_copy(k, s):
        count = both if s == 0 else (pairs - 1 - s) * group
        return pltpu.make_async_remote_copy(
            src_ref=raw.at[k] if s == 0 else rout.at[k, pl.ds(0, count)],
            dst_ref=rin.at[k, pl.ds(0, count)],
            send_sem=rt_s.at[k], recv_sem=rt_r.at[k],
            device_id=(2 * (s + 1) + core, brick), device_id_type=MESH)

    def left_copy(k, s):
        count = both if s == pairs - 1 else s * group
        return pltpu.make_async_remote_copy(
            src_ref=raw.at[k] if s == pairs - 1 else lout.at[k, pl.ds(0, count)],
            dst_ref=lin.at[k, pl.ds(0, count)],
            send_sem=lt_s.at[k], recv_sem=lt_r.at[k],
            device_id=(2 * (s - 1) + core, brick), device_id_type=MESH)

    def fin_copy(k):
        return pltpu.make_async_remote_copy(
            src_ref=own.at[k, pl.ds((1 - core) * per_dev, per_dev)], dst_ref=fin.at[k],
            send_sem=fin_s.at[k], recv_sem=fin_r.at[k],
            device_id=(sib, brick), device_id_type=MESH)

    def weighted(buf, k, r, source_pair):
        starts = [((r + i) * shots + 2 * source_pair) * BLOCKS for i in range(WIDTH)]
        block = buf[k, 0]
        totals = [wt_ref[start] * block for start in starts]
        for q in range(1, both):
            block = buf[k, q]
            totals = [total + wt_ref[start + q] * block for total, start in zip(totals, starts)]
        return totals

    def plus(totals, terms):
        return [total + term for total, term in zip(totals, terms)]

    def entries(buf, k, q):
        return [buf[k, q + i] for i in range(WIDTH)]

    def produce(k):
        @pl.when(brick > 0)
        def _():
            pltpu.make_async_remote_copy(
                src_ref=hs_up.at[k], dst_ref=h_before.at[k], send_sem=up_s.at[k], recv_sem=up_r.at[k],
                device_id=(shot, brick - 1), device_id_type=MESH).wait_recv()

        @pl.when(brick < bricks - 1)
        def _():
            pltpu.make_async_remote_copy(
                src_ref=hs_dn.at[k], dst_ref=h_after.at[k], send_sem=dn_s.at[k], recv_sem=dn_r.at[k],
                device_id=(shot, brick + 1), device_id_type=MESH).wait_recv()

        def images(b, side):
            return [(b + i, r, image(k, 2 * (b + i) + side, r)) for i in range(2) for r in range(ROWS)]

        def other(step, carry):
            for b, r, value in images(2 * step, 1 - core):
                gsend[k, b, r] = value
            return carry

        lax.fori_loop(0, BLOCKS // 2, other, 0)
        sib_copy(k).start()

        def mine(step, carry):
            for b, r, value in images(2 * step, core):
                raw[k, core * BLOCKS + b, r] = value
            return carry

        lax.fori_loop(0, BLOCKS // 2, mine, 0)

    def right_flow(k):
        for s in range(pairs - 1):
            @pl.when(pair == s + 1)
            def _(s=s):
                right_copy(k, s).wait_recv()

        for s in range(pairs - 1):
            @pl.when(pair == s)
            def _(s=s):
                if s > 0:
                    def body(step, carry):
                        q = step * WIDTH
                        r = (s + 1) * group + q
                        totals = weighted(raw, k, r, s)
                        if s == 1:
                            totals = plus(totals, weighted(rin, k, r, 0))
                        else:
                            totals = plus(totals, entries(rin, k, q + group))
                        for i in range(WIDTH):
                            rout[k, q + i] = totals[i]
                        return carry

                    lax.fori_loop(0, (pairs - 1 - s) * group // WIDTH, body, 0)
                right_copy(k, s).start()

    def left_flow(k):
        for s in range(1, pairs):
            @pl.when(pair == s - 1)
            def _(s=s):
                left_copy(k, s).wait_recv()

        for s in range(1, pairs):
            @pl.when(pair == s)
            def _(s=s):
                if s < pairs - 1:
                    def body(step, carry):
                        q = step * WIDTH
                        totals = weighted(raw, k, q, s)
                        if s == pairs - 2:
                            totals = plus(totals, weighted(lin, k, q, pairs - 1))
                        else:
                            totals = plus(totals, entries(lin, k, q))
                        for i in range(WIDTH):
                            lout[k, q + i] = totals[i]
                        return carry

                    lax.fori_loop(0, s * group // WIDTH, body, 0)
                left_copy(k, s).start()

    def finish(k):
        for s in range(pairs):
            @pl.when(pair == s)
            def _(s=s):
                def body(step, carry):
                    q = step * WIDTH
                    r = s * group + q
                    totals = weighted(raw, k, r, s)
                    if s == 1:
                        totals = plus(totals, weighted(rin, k, r, 0))
                    elif s > 1:
                        totals = plus(totals, entries(rin, k, q))
                    if s == pairs - 2:
                        totals = plus(totals, weighted(lin, k, r, pairs - 1))
                    elif s < pairs - 1:
                        totals = plus(totals, entries(lin, k, s * group + q))
                    for i in range(WIDTH):
                        own[k, q + i] = totals[i]
                    return carry

                lax.fori_loop(0, group // WIDTH, body, 0)

        fin_copy(k).start()
        for q in range(per_dev):
            out_ref[q, core, k] = own[k, core * per_dev + q]

    near_lag, far_lag, end_lag = 1, 2, 3
    is_left = pair < pairs // 2
    right_lag = jnp.where(is_left, near_lag, far_lag)
    left_lag = jnp.where(is_left, far_lag, near_lag)

    def step(t, carry):
        @pl.when(t < chunks)
        def _():
            produce(t)

        @pl.when((t >= 1) & (t < chunks + 1))
        def _():
            sib_wait(t - 1)

        kr = t - right_lag
        kl = t - left_lag

        @pl.when((kr >= 0) & (kr < chunks))
        def _():
            right_flow(kr)

        @pl.when((kl >= 0) & (kl < chunks))
        def _():
            left_flow(kl)

        @pl.when(t >= end_lag)
        def _():
            finish(t - end_lag)

        return carry

    lax.fori_loop(0, chunks + end_lag, step, 0)

    def drain(k, carry):
        fin_copy(k).wait_recv()
        for q in range(per_dev):
            out_ref[q, 1 - core, k] = fin[k, q]
        fin_copy(k).wait_send()
        sib_copy(k).wait_send()

        @pl.when(brick < bricks - 1)
        def _():
            up_copy(k).wait_send()

        @pl.when(brick > 0)
        def _():
            dn_copy(k).wait_send()

        for s in range(pairs - 1):
            @pl.when(pair == s)
            def _(s=s):
                right_copy(k, s).wait_send()

            @pl.when(pair == s + 1)
            def _(s=s):
                left_copy(k, s + 1).wait_send()

        return carry

    lax.fori_loop(0, chunks, drain, 0)


def sine_taper(count, extent):
    positions = jnp.arange(count, dtype=jnp.int32).astype(jnp.float32)
    return jnp.sin(jnp.pi * (positions + 0.5) / extent)


def per_device(shots, bricks, sources, slowness, group_size, window_anchor, tile_slot):
    wide_y, planes, wide_z = slowness.shape[1:]
    half_rows = wide_y // (2 * BLOCKS)
    chunks = half_rows // ROWS
    brick_index = lax.axis_index("brick")
    shot_index = lax.axis_index("shot")
    tiles = tile_slot.shape[0]
    per_dev = tiles // shots
    pairs = shots // 2
    group = 2 * per_dev
    both = 2 * BLOCKS

    extent = group_size[shot_index] * planes
    depth_ids = brick_index * planes + jnp.arange(planes, dtype=jnp.int32)
    active = depth_ids < extent
    mask = (brick_index < group_size[shot_index]).astype(jnp.float32).reshape(1)
    taper_x = jnp.where(
        active,
        jnp.sin(jnp.pi * (depth_ids.astype(jnp.float32) + 0.5) / extent.astype(jnp.float32)),
        0.0,
    )
    taper_xz = taper_x[:, None] * sine_taper(wide_z, float(wide_z))[None, :]
    taper_y = sine_taper(wide_y, float(wide_y))
    piece_slots = tile_slot[window_anchor[:, None] + jnp.arange(BLOCKS, dtype=jnp.int32)[None, :]]
    slots = jnp.arange(tiles, dtype=jnp.int32)
    weights = (slots[:, None, None] == piece_slots[None]).astype(jnp.float32).reshape(-1)

    chunk = (ROWS, planes, wide_z)
    src = sources.reshape((4, 2 * BLOCKS, chunks) + chunk)
    slow = slowness.reshape((2 * BLOCKS, chunks) + chunk)
    f32 = jnp.float32
    wide = max(both, (pairs - 2) * group)
    fwd = max(group, (pairs - 2) * group)
    dma = pltpu.SemaphoreType.DMA
    smem = pl.BlockSpec(memory_space=pltpu.SMEM)
    vmem = pl.BlockSpec(memory_space=pltpu.VMEM)
    hbm = pl.BlockSpec(memory_space=pl.ANY)
    halo = pltpu.VMEM((chunks, 4, both * ROWS, wide_z), f32)
    out = pl.pallas_call(
        functools.partial(kernel, shots, bricks, per_dev, chunks),
        out_shape=jax.ShapeDtypeStruct((per_dev, 2, chunks) + chunk, f32),
        in_specs=[smem, smem, smem, vmem, hbm, hbm],
        out_specs=vmem,
        scratch_shapes=[
            pltpu.VMEM((2, 4, both) + chunk, f32),
            pltpu.VMEM((2, both) + chunk, f32),
            pltpu.VMEM((4, wide_y + 2, planes, wide_z), f32),
            pltpu.VMEM((2, wide_y, planes, wide_z), f32),
            halo, halo, halo, halo,
            pltpu.VMEM((chunks, BLOCKS) + chunk, f32),
            pltpu.VMEM((chunks, both) + chunk, f32),
            pltpu.VMEM((chunks, wide) + chunk, f32),
            pltpu.VMEM((chunks, fwd) + chunk, f32),
            pltpu.VMEM((chunks, wide) + chunk, f32),
            pltpu.VMEM((chunks, fwd) + chunk, f32),
            pltpu.VMEM((chunks, group) + chunk, f32),
            pltpu.VMEM((chunks, per_dev) + chunk, f32),
            dma((2,)), dma((2,)),
        ] + [dma((chunks,))] * 12,
        compiler_params=pltpu.CompilerParams(
            collective_id=0, has_side_effects=True, vmem_limit_bytes=62 * 1024 * 1024
        ),
        cost_estimate=pl.CostEstimate(
            flops=200 * wide_y * planes * wide_z, bytes_accessed=12 * 1024 * 1024, transcendentals=0
        ),
    )(mask, taper_y, weights, taper_xz, src, slow)
    return out.reshape(1, per_dev, -1)


def solution(mesh):
    return jax.shard_map(
        functools.partial(per_device, mesh.shape["shot"], mesh.shape["brick"]),
        mesh=mesh,
        in_specs=(
            P("shot", None, None, None, "brick", None),
            P("shot", None, "brick", None),
            P(),
            P(),
            P(),
        ),
        out_specs=P("brick", "shot", None),
        check_vma=False,
    )
```

```python
import functools

import jax
import jax.numpy as jnp
from jax import lax
from jax.experimental import pallas as pl
from jax.experimental.pallas import tpu as pltpu
from jax.sharding import PartitionSpec as P

BLOCKS = 8
WIDTH = 8
ROWS = 1
MESH = pl.DeviceIdType.MESH

shift_beta = 0.5
relaxation = 0.8


def kernel(
    shots, bricks, per_dev, chunks,
    mask_ref, ty_ref, wt_ref, txz_ref, src_ref, slow_ref,
    out_ref,
    sbuf, wbuf, f1, inv, hs_up, hs_dn, h_before, h_after, gsend, raw,
    rin, rout, lin, lout, own, fin,
    in_sem, win_sem, up_s, up_r, dn_s, dn_r, sib_s, sib_r, rt_s, rt_r, lt_s, lt_r, fin_s, fin_r,
):
    shot = lax.axis_index("shot")
    brick = lax.axis_index("brick")
    pair, core = shot // 2, shot % 2
    sib = pair * 2 + (1 - core)
    pairs = shots // 2
    group = 2 * per_dev
    both = 2 * BLOCKS
    half_rows = chunks * ROWS
    wide_y = 2 * BLOCKS * half_rows

    def source_copies(k, slot):
        return (
            pltpu.make_async_copy(src_ref.at[:, :, k], sbuf.at[slot], in_sem.at[slot]),
            pltpu.make_async_copy(slow_ref.at[:, k], wbuf.at[slot], win_sem.at[slot]),
        )

    for copy in source_copies(0, 0):
        copy.start()

    barrier = pltpu.get_barrier_semaphore()

    def greet(s, b):
        pl.semaphore_signal(barrier, inc=1, device_id=(s, b), device_id_type=MESH)

    greet(sib, brick)

    @pl.when(brick > 0)
    def _():
        greet(shot, brick - 1)

    @pl.when(brick < bricks - 1)
    def _():
        greet(shot, brick + 1)

    @pl.when(pair > 0)
    def _():
        greet(shot - 2, brick)

    @pl.when(pair < pairs - 1)
    def _():
        greet(shot + 2, brick)

    @pl.when(brick == 0)
    def _():
        h_before[...] = jnp.zeros_like(h_before)

    @pl.when(brick == bricks - 1)
    def _():
        h_after[...] = jnp.zeros_like(h_after)

    zero_row = jnp.zeros((1,) + f1.shape[2:], jnp.float32)
    for c in range(4):
        f1[c, pl.ds(0, 1)] = zero_row
        f1[c, pl.ds(wide_y + 1, 1)] = zero_row

    one = jnp.int32(1)
    nothing = jnp.int32(0)
    friends = (
        one
        + jnp.where(brick > 0, one, nothing)
        + jnp.where(brick < bricks - 1, one, nothing)
        + jnp.where(pair > 0, one, nothing)
        + jnp.where(pair < pairs - 1, one, nothing)
    )
    pl.semaphore_wait(barrier, friends)

    def up_copy(k):
        return pltpu.make_async_remote_copy(
            src_ref=hs_up.at[k], dst_ref=h_before.at[k], send_sem=up_s.at[k], recv_sem=up_r.at[k],
            device_id=(shot, brick + 1), device_id_type=MESH)

    def dn_copy(k):
        return pltpu.make_async_remote_copy(
            src_ref=hs_dn.at[k], dst_ref=h_after.at[k], send_sem=dn_s.at[k], recv_sem=dn_r.at[k],
            device_id=(shot, brick - 1), device_id_type=MESH)

    mask = mask_ref[0]

    def first(k, carry):
        slot = lax.rem(k, 2)

        @pl.when(k + 1 < chunks)
        def _():
            for copy in source_copies(k + 1, 1 - slot):
                copy.start()

        for copy in source_copies(k, slot):
            copy.wait()

        def rows(j, carry):
            y = j * half_rows + k * ROWS
            w = wbuf[slot, j]
            real_d = 6.0 - w
            imag_d = shift_beta * w
            scale = relaxation / (real_d * real_d + imag_d * imag_d)
            ire = real_d * scale
            iim = imag_d * scale
            inv[0, pl.ds(y, ROWS)] = ire
            inv[1, pl.ds(y, ROWS)] = iim
            mre, mim = ire * mask, iim * mask
            fields = []
            for p in range(2):
                a, b = sbuf[slot, 2 * p, j], sbuf[slot, 2 * p + 1, j]
                fields += [a * mre - b * mim, a * mim + b * mre]
            for c, f in enumerate(fields):
                f1[c, pl.ds(y + 1, ROWS)] = f
                for r in range(ROWS):
                    hs_dn[k, c, pl.ds(j * ROWS + r, 1), :] = f[r, 0:1, :]
                    hs_up[k, c, pl.ds(j * ROWS + r, 1), :] = f[r, 7:8, :]
            return carry

        lax.fori_loop(0, both, rows, 0)

        @pl.when(brick < bricks - 1)
        def _():
            up_copy(k).start()

        @pl.when(brick > 0)
        def _():
            dn_copy(k).start()

        return carry

    lax.fori_loop(0, chunks, first, 0)

    planes, wide_z = f1.shape[2:]
    lane = lax.broadcasted_iota(jnp.int32, (planes, wide_z), 1)
    sub = lax.broadcasted_iota(jnp.int32, (planes, wide_z), 0)

    def image(k, j, r):
        y = j * half_rows + k * ROWS + r
        hrow = j * ROWS + r
        centre, near = [], []
        for c in range(4):
            f = f1[c, y + 1]
            total = f1[c, y] + f1[c, y + 2]
            total += jnp.where(lane == 0, 0.0, pltpu.roll(f, 1, axis=1))
            total += jnp.where(lane == wide_z - 1, 0.0, pltpu.roll(f, wide_z - 1, axis=1))
            total += jnp.where(sub == 0, h_before[k, c, pl.ds(hrow, 1), :], pltpu.roll(f, 1, axis=0))
            total += jnp.where(sub == planes - 1, h_after[k, c, pl.ds(hrow, 1), :], pltpu.roll(f, planes - 1, axis=0))
            centre.append(f)
            near.append(total)
        ire, iim = inv[0, y], inv[1, y]
        keep = 2.0 - relaxation
        field = []
        for p in (0, 2):
            field.append(keep * centre[p] + (near[p] * ire - near[p + 1] * iim))
            field.append(keep * centre[p + 1] + (near[p] * iim + near[p + 1] * ire))
        imaging = (
            field[0] * field[2]
            - field[1] * field[3]
            - shift_beta * (field[0] * field[3] + field[1] * field[2])
        )
        return imaging * (txz_ref[...] * ty_ref[y])

    def sib_copy(k):
        return pltpu.make_async_remote_copy(
            src_ref=gsend.at[k], dst_ref=raw.at[k, pl.ds(core * BLOCKS, BLOCKS)],
            send_sem=sib_s.at[k], recv_sem=sib_r.at[k],
            device_id=(sib, brick), device_id_type=MESH)

    def sib_wait(k):
        pltpu.make_async_remote_copy(
            src_ref=gsend.at[k], dst_ref=raw.at[k, pl.ds((1 - core) * BLOCKS, BLOCKS)],
            send_sem=sib_s.at[k], recv_sem=sib_r.at[k],
            device_id=(sib, brick), device_id_type=MESH).wait_recv()

    def right_copy(k, s):
        count = both if s == 0 else (pairs - 1 - s) * group
        return pltpu.make_async_remote_copy(
            src_ref=raw.at[k] if s == 0 else rout.at[k, pl.ds(0, count)],
            dst_ref=rin.at[k, pl.ds(0, count)],
            send_sem=rt_s.at[k], recv_sem=rt_r.at[k],
            device_id=(2 * (s + 1) + core, brick), device_id_type=MESH)

    def left_copy(k, s):
        count = both if s == pairs - 1 else s * group
        return pltpu.make_async_remote_copy(
            src_ref=raw.at[k] if s == pairs - 1 else lout.at[k, pl.ds(0, count)],
            dst_ref=lin.at[k, pl.ds(0, count)],
            send_sem=lt_s.at[k], recv_sem=lt_r.at[k],
            device_id=(2 * (s - 1) + core, brick), device_id_type=MESH)

    def fin_copy(k):
        return pltpu.make_async_remote_copy(
            src_ref=own.at[k, pl.ds((1 - core) * per_dev, per_dev)], dst_ref=fin.at[k],
            send_sem=fin_s.at[k], recv_sem=fin_r.at[k],
            device_id=(sib, brick), device_id_type=MESH)

    def weighted(buf, k, r, source_pair):
        starts = [((r + i) * shots + 2 * source_pair) * BLOCKS for i in range(WIDTH)]
        block = buf[k, 0]
        totals = [wt_ref[start] * block for start in starts]
        for q in range(1, both):
            block = buf[k, q]
            totals = [total + wt_ref[start + q] * block for total, start in zip(totals, starts)]
        return totals

    def plus(totals, terms):
        return [total + term for total, term in zip(totals, terms)]

    def entries(buf, k, q):
        return [buf[k, q + i] for i in range(WIDTH)]

    def produce(k):
        @pl.when(brick > 0)
        def _():
            pltpu.make_async_remote_copy(
                src_ref=hs_up.at[k], dst_ref=h_before.at[k], send_sem=up_s.at[k], recv_sem=up_r.at[k],
                device_id=(shot, brick - 1), device_id_type=MESH).wait_recv()

        @pl.when(brick < bricks - 1)
        def _():
            pltpu.make_async_remote_copy(
                src_ref=hs_dn.at[k], dst_ref=h_after.at[k], send_sem=dn_s.at[k], recv_sem=dn_r.at[k],
                device_id=(shot, brick + 1), device_id_type=MESH).wait_recv()

        def images(b, side):
            return [(b + i, r, image(k, 2 * (b + i) + side, r)) for i in range(4) for r in range(ROWS)]

        def other(step, carry):
            for b, r, value in images(4 * step, 1 - core):
                gsend[k, b, r] = value
            return carry

        lax.fori_loop(0, BLOCKS // 4, other, 0)
        sib_copy(k).start()

        def mine(step, carry):
            for b, r, value in images(4 * step, core):
                raw[k, core * BLOCKS + b, r] = value
            return carry

        lax.fori_loop(0, BLOCKS // 4, mine, 0)

    def right_flow(k):
        for s in range(pairs - 1):
            @pl.when(pair == s + 1)
            def _(s=s):
                right_copy(k, s).wait_recv()

        for s in range(pairs - 1):
            @pl.when(pair == s)
            def _(s=s):
                if s > 0:
                    def body(step, carry):
                        q = step * WIDTH
                        r = (s + 1) * group + q
                        totals = weighted(raw, k, r, s)
                        if s == 1:
                            totals = plus(totals, weighted(rin, k, r, 0))
                        else:
                            totals = plus(totals, entries(rin, k, q + group))
                        for i in range(WIDTH):
                            rout[k, q + i] = totals[i]
                        return carry

                    lax.fori_loop(0, (pairs - 1 - s) * group // WIDTH, body, 0)
                right_copy(k, s).start()

    def left_flow(k):
        for s in range(1, pairs):
            @pl.when(pair == s - 1)
            def _(s=s):
                left_copy(k, s).wait_recv()

        for s in range(1, pairs):
            @pl.when(pair == s)
            def _(s=s):
                if s < pairs - 1:
                    def body(step, carry):
                        q = step * WIDTH
                        totals = weighted(raw, k, q, s)
                        if s == pairs - 2:
                            totals = plus(totals, weighted(lin, k, q, pairs - 1))
                        else:
                            totals = plus(totals, entries(lin, k, q))
                        for i in range(WIDTH):
                            lout[k, q + i] = totals[i]
                        return carry

                    lax.fori_loop(0, s * group // WIDTH, body, 0)
                left_copy(k, s).start()

    def finish(k):
        for s in range(pairs):
            @pl.when(pair == s)
            def _(s=s):
                def body(step, carry):
                    q = step * WIDTH
                    r = s * group + q
                    totals = weighted(raw, k, r, s)
                    if s == 1:
                        totals = plus(totals, weighted(rin, k, r, 0))
                    elif s > 1:
                        totals = plus(totals, entries(rin, k, q))
                    if s == pairs - 2:
                        totals = plus(totals, weighted(lin, k, r, pairs - 1))
                    elif s < pairs - 1:
                        totals = plus(totals, entries(lin, k, s * group + q))
                    for i in range(WIDTH):
                        own[k, q + i] = totals[i]
                    return carry

                lax.fori_loop(0, group // WIDTH, body, 0)

        fin_copy(k).start()
        for q in range(per_dev):
            out_ref[q, core, k] = own[k, core * per_dev + q]

    near_lag, far_lag, end_lag = 1, 2, 3
    is_left = pair < pairs // 2
    right_lag = jnp.where(is_left, near_lag, far_lag)
    left_lag = jnp.where(is_left, far_lag, near_lag)

    def step(t, carry):
        @pl.when(t < chunks)
        def _():
            produce(t)

        @pl.when((t >= 1) & (t < chunks + 1))
        def _():
            sib_wait(t - 1)

        kr = t - right_lag
        kl = t - left_lag

        @pl.when((kr >= 0) & (kr < chunks))
        def _():
            right_flow(kr)

        @pl.when((kl >= 0) & (kl < chunks))
        def _():
            left_flow(kl)

        @pl.when(t >= end_lag)
        def _():
            finish(t - end_lag)

        return carry

    lax.fori_loop(0, chunks + end_lag, step, 0)

    def drain(k, carry):
        fin_copy(k).wait_recv()
        for q in range(per_dev):
            out_ref[q, 1 - core, k] = fin[k, q]
        fin_copy(k).wait_send()
        sib_copy(k).wait_send()

        @pl.when(brick < bricks - 1)
        def _():
            up_copy(k).wait_send()

        @pl.when(brick > 0)
        def _():
            dn_copy(k).wait_send()

        for s in range(pairs - 1):
            @pl.when(pair == s)
            def _(s=s):
                right_copy(k, s).wait_send()

            @pl.when(pair == s + 1)
            def _(s=s):
                left_copy(k, s + 1).wait_send()

        return carry

    lax.fori_loop(0, chunks, drain, 0)


def sine_taper(count, extent):
    positions = jnp.arange(count, dtype=jnp.int32).astype(jnp.float32)
    return jnp.sin(jnp.pi * (positions + 0.5) / extent)


def per_device(shots, bricks, sources, slowness, group_size, window_anchor, tile_slot):
    wide_y, planes, wide_z = slowness.shape[1:]
    half_rows = wide_y // (2 * BLOCKS)
    chunks = half_rows // ROWS
    brick_index = lax.axis_index("brick")
    shot_index = lax.axis_index("shot")
    tiles = tile_slot.shape[0]
    per_dev = tiles // shots
    pairs = shots // 2
    group = 2 * per_dev
    both = 2 * BLOCKS

    extent = group_size[shot_index] * planes
    depth_ids = brick_index * planes + jnp.arange(planes, dtype=jnp.int32)
    active = depth_ids < extent
    mask = (brick_index < group_size[shot_index]).astype(jnp.float32).reshape(1)
    taper_x = jnp.where(
        active,
        jnp.sin(jnp.pi * (depth_ids.astype(jnp.float32) + 0.5) / extent.astype(jnp.float32)),
        0.0,
    )
    taper_xz = taper_x[:, None] * sine_taper(wide_z, float(wide_z))[None, :]
    taper_y = sine_taper(wide_y, float(wide_y))
    piece_slots = tile_slot[window_anchor[:, None] + jnp.arange(BLOCKS, dtype=jnp.int32)[None, :]]
    slots = jnp.arange(tiles, dtype=jnp.int32)
    weights = (slots[:, None, None] == piece_slots[None]).astype(jnp.float32).reshape(-1)

    chunk = (ROWS, planes, wide_z)
    src = sources.reshape((4, 2 * BLOCKS, chunks) + chunk)
    slow = slowness.reshape((2 * BLOCKS, chunks) + chunk)
    f32 = jnp.float32
    wide = max(both, (pairs - 2) * group)
    fwd = max(group, (pairs - 2) * group)
    dma = pltpu.SemaphoreType.DMA
    smem = pl.BlockSpec(memory_space=pltpu.SMEM)
    vmem = pl.BlockSpec(memory_space=pltpu.VMEM)
    hbm = pl.BlockSpec(memory_space=pl.ANY)
    halo = pltpu.VMEM((chunks, 4, both * ROWS, wide_z), f32)
    out = pl.pallas_call(
        functools.partial(kernel, shots, bricks, per_dev, chunks),
        out_shape=jax.ShapeDtypeStruct((per_dev, 2, chunks) + chunk, f32),
        in_specs=[smem, smem, smem, vmem, hbm, hbm],
        out_specs=vmem,
        scratch_shapes=[
            pltpu.VMEM((2, 4, both) + chunk, f32),
            pltpu.VMEM((2, both) + chunk, f32),
            pltpu.VMEM((4, wide_y + 2, planes, wide_z), f32),
            pltpu.VMEM((2, wide_y, planes, wide_z), f32),
            halo, halo, halo, halo,
            pltpu.VMEM((chunks, BLOCKS) + chunk, f32),
            pltpu.VMEM((chunks, both) + chunk, f32),
            pltpu.VMEM((chunks, wide) + chunk, f32),
            pltpu.VMEM((chunks, fwd) + chunk, f32),
            pltpu.VMEM((chunks, wide) + chunk, f32),
            pltpu.VMEM((chunks, fwd) + chunk, f32),
            pltpu.VMEM((chunks, group) + chunk, f32),
            pltpu.VMEM((chunks, per_dev) + chunk, f32),
            dma((2,)), dma((2,)),
        ] + [dma((chunks,))] * 12,
        compiler_params=pltpu.CompilerParams(
            collective_id=0, has_side_effects=True, vmem_limit_bytes=62 * 1024 * 1024
        ),
        cost_estimate=pl.CostEstimate(
            flops=200 * wide_y * planes * wide_z, bytes_accessed=12 * 1024 * 1024, transcendentals=0
        ),
    )(mask, taper_y, weights, taper_xz, src, slow)
    return out.reshape(1, per_dev, -1)


def solution(mesh):
    return jax.shard_map(
        functools.partial(per_device, mesh.shape["shot"], mesh.shape["brick"]),
        mesh=mesh,
        in_specs=(
            P("shot", None, None, None, "brick", None),
            P("shot", None, "brick", None),
            P(),
            P(),
            P(),
        ),
        out_specs=P("brick", "shot", None),
        check_vma=False,
    )
```

```python
import functools

import jax
import jax.numpy as jnp
from jax import lax
from jax.experimental import pallas as pl
from jax.experimental.pallas import tpu as pltpu
from jax.sharding import PartitionSpec as P

BLOCKS = 8
WIDTH = 2
ROWS = 4
MESH = pl.DeviceIdType.MESH

shift_beta = 0.5
relaxation = 0.8


def kernel(
    shots, bricks, per_dev, chunks,
    mask_ref, ty_ref, wt_ref, txz_ref, src_ref, slow_ref,
    out_ref,
    sbuf, wbuf, f1, inv, hs_up, hs_dn, h_before, h_after, gsend, raw,
    rin, rout, lin, lout, own, fin,
    in_sem, win_sem, up_s, up_r, dn_s, dn_r, sib_s, sib_r, rt_s, rt_r, lt_s, lt_r, fin_s, fin_r,
):
    shot = lax.axis_index("shot")
    brick = lax.axis_index("brick")
    pair, core = shot // 2, shot % 2
    sib = pair * 2 + (1 - core)
    pairs = shots // 2
    group = 2 * per_dev
    both = 2 * BLOCKS
    half_rows = chunks * ROWS
    wide_y = 2 * BLOCKS * half_rows

    def source_copies(k, slot):
        return (
            pltpu.make_async_copy(src_ref.at[:, :, k], sbuf.at[slot], in_sem.at[slot]),
            pltpu.make_async_copy(slow_ref.at[:, k], wbuf.at[slot], win_sem.at[slot]),
        )

    for copy in source_copies(0, 0):
        copy.start()

    barrier = pltpu.get_barrier_semaphore()

    def greet(s, b):
        pl.semaphore_signal(barrier, inc=1, device_id=(s, b), device_id_type=MESH)

    greet(sib, brick)

    @pl.when(brick > 0)
    def _():
        greet(shot, brick - 1)

    @pl.when(brick < bricks - 1)
    def _():
        greet(shot, brick + 1)

    @pl.when(pair > 0)
    def _():
        greet(shot - 2, brick)

    @pl.when(pair < pairs - 1)
    def _():
        greet(shot + 2, brick)

    @pl.when(brick == 0)
    def _():
        h_before[...] = jnp.zeros_like(h_before)

    @pl.when(brick == bricks - 1)
    def _():
        h_after[...] = jnp.zeros_like(h_after)

    zero_row = jnp.zeros((1,) + f1.shape[2:], jnp.float32)
    for c in range(4):
        f1[c, pl.ds(0, 1)] = zero_row
        f1[c, pl.ds(wide_y + 1, 1)] = zero_row

    one = jnp.int32(1)
    nothing = jnp.int32(0)
    friends = (
        one
        + jnp.where(brick > 0, one, nothing)
        + jnp.where(brick < bricks - 1, one, nothing)
        + jnp.where(pair > 0, one, nothing)
        + jnp.where(pair < pairs - 1, one, nothing)
    )
    pl.semaphore_wait(barrier, friends)

    def up_copy(k):
        return pltpu.make_async_remote_copy(
            src_ref=hs_up.at[k], dst_ref=h_before.at[k], send_sem=up_s.at[k], recv_sem=up_r.at[k],
            device_id=(shot, brick + 1), device_id_type=MESH)

    def dn_copy(k):
        return pltpu.make_async_remote_copy(
            src_ref=hs_dn.at[k], dst_ref=h_after.at[k], send_sem=dn_s.at[k], recv_sem=dn_r.at[k],
            device_id=(shot, brick - 1), device_id_type=MESH)

    mask = mask_ref[0]

    def first(k, carry):
        slot = lax.rem(k, 2)

        @pl.when(k + 1 < chunks)
        def _():
            for copy in source_copies(k + 1, 1 - slot):
                copy.start()

        for copy in source_copies(k, slot):
            copy.wait()

        def rows(j, carry):
            y = j * half_rows + k * ROWS
            w = wbuf[slot, j]
            real_d = 6.0 - w
            imag_d = shift_beta * w
            scale = relaxation / (real_d * real_d + imag_d * imag_d)
            ire = real_d * scale
            iim = imag_d * scale
            inv[0, pl.ds(y, ROWS)] = ire
            inv[1, pl.ds(y, ROWS)] = iim
            mre, mim = ire * mask, iim * mask
            fields = []
            for p in range(2):
                a, b = sbuf[slot, 2 * p, j], sbuf[slot, 2 * p + 1, j]
                fields += [a * mre - b * mim, a * mim + b * mre]
            for c, f in enumerate(fields):
                f1[c, pl.ds(y + 1, ROWS)] = f
                for r in range(ROWS):
                    hs_dn[k, c, pl.ds(j * ROWS + r, 1), :] = f[r, 0:1, :]
                    hs_up[k, c, pl.ds(j * ROWS + r, 1), :] = f[r, 7:8, :]
            return carry

        lax.fori_loop(0, both, rows, 0)

        @pl.when(brick < bricks - 1)
        def _():
            up_copy(k).start()

        @pl.when(brick > 0)
        def _():
            dn_copy(k).start()

        return carry

    lax.fori_loop(0, chunks, first, 0)

    planes, wide_z = f1.shape[2:]
    lane = lax.broadcasted_iota(jnp.int32, (planes, wide_z), 1)
    sub = lax.broadcasted_iota(jnp.int32, (planes, wide_z), 0)

    def image(k, j, r):
        y = j * half_rows + k * ROWS + r
        hrow = j * ROWS + r
        centre, near = [], []
        for c in range(4):
            f = f1[c, y + 1]
            total = f1[c, y] + f1[c, y + 2]
            total += jnp.where(lane == 0, 0.0, pltpu.roll(f, 1, axis=1))
            total += jnp.where(lane == wide_z - 1, 0.0, pltpu.roll(f, wide_z - 1, axis=1))
            total += jnp.where(sub == 0, h_before[k, c, pl.ds(hrow, 1), :], pltpu.roll(f, 1, axis=0))
            total += jnp.where(sub == planes - 1, h_after[k, c, pl.ds(hrow, 1), :], pltpu.roll(f, planes - 1, axis=0))
            centre.append(f)
            near.append(total)
        ire, iim = inv[0, y], inv[1, y]
        keep = 2.0 - relaxation
        field = []
        for p in (0, 2):
            field.append(keep * centre[p] + (near[p] * ire - near[p + 1] * iim))
            field.append(keep * centre[p + 1] + (near[p] * iim + near[p + 1] * ire))
        imaging = (
            field[0] * field[2]
            - field[1] * field[3]
            - shift_beta * (field[0] * field[3] + field[1] * field[2])
        )
        return imaging * (txz_ref[...] * ty_ref[y])

    def sib_copy(k):
        return pltpu.make_async_remote_copy(
            src_ref=gsend.at[k], dst_ref=raw.at[k, pl.ds(core * BLOCKS, BLOCKS)],
            send_sem=sib_s.at[k], recv_sem=sib_r.at[k],
            device_id=(sib, brick), device_id_type=MESH)

    def sib_wait(k):
        pltpu.make_async_remote_copy(
            src_ref=gsend.at[k], dst_ref=raw.at[k, pl.ds((1 - core) * BLOCKS, BLOCKS)],
            send_sem=sib_s.at[k], recv_sem=sib_r.at[k],
            device_id=(sib, brick), device_id_type=MESH).wait_recv()

    def right_copy(k, s):
        count = both if s == 0 else (pairs - 1 - s) * group
        return pltpu.make_async_remote_copy(
            src_ref=raw.at[k] if s == 0 else rout.at[k, pl.ds(0, count)],
            dst_ref=rin.at[k, pl.ds(0, count)],
            send_sem=rt_s.at[k], recv_sem=rt_r.at[k],
            device_id=(2 * (s + 1) + core, brick), device_id_type=MESH)

    def left_copy(k, s):
        count = both if s == pairs - 1 else s * group
        return pltpu.make_async_remote_copy(
            src_ref=raw.at[k] if s == pairs - 1 else lout.at[k, pl.ds(0, count)],
            dst_ref=lin.at[k, pl.ds(0, count)],
            send_sem=lt_s.at[k], recv_sem=lt_r.at[k],
            device_id=(2 * (s - 1) + core, brick), device_id_type=MESH)

    def fin_copy(k):
        return pltpu.make_async_remote_copy(
            src_ref=own.at[k, pl.ds((1 - core) * per_dev, per_dev)], dst_ref=fin.at[k],
            send_sem=fin_s.at[k], recv_sem=fin_r.at[k],
            device_id=(sib, brick), device_id_type=MESH)

    def weighted(buf, k, r, source_pair):
        starts = [((r + i) * shots + 2 * source_pair) * BLOCKS for i in range(WIDTH)]
        block = buf[k, 0]
        totals = [wt_ref[start] * block for start in starts]
        for q in range(1, both):
            block = buf[k, q]
            totals = [total + wt_ref[start + q] * block for total, start in zip(totals, starts)]
        return totals

    def plus(totals, terms):
        return [total + term for total, term in zip(totals, terms)]

    def entries(buf, k, q):
        return [buf[k, q + i] for i in range(WIDTH)]

    def produce(k):
        @pl.when(brick > 0)
        def _():
            pltpu.make_async_remote_copy(
                src_ref=hs_up.at[k], dst_ref=h_before.at[k], send_sem=up_s.at[k], recv_sem=up_r.at[k],
                device_id=(shot, brick - 1), device_id_type=MESH).wait_recv()

        @pl.when(brick < bricks - 1)
        def _():
            pltpu.make_async_remote_copy(
                src_ref=hs_dn.at[k], dst_ref=h_after.at[k], send_sem=dn_s.at[k], recv_sem=dn_r.at[k],
                device_id=(shot, brick + 1), device_id_type=MESH).wait_recv()

        def images(b, side):
            return [(b + i, r, image(k, 2 * (b + i) + side, r)) for i in range(1) for r in range(ROWS)]

        def other(step, carry):
            for b, r, value in images(step, 1 - core):
                gsend[k, b, r] = value
            return carry

        lax.fori_loop(0, BLOCKS, other, 0)
        sib_copy(k).start()

        def mine(step, carry):
            for b, r, value in images(step, core):
                raw[k, core * BLOCKS + b, r] = value
            return carry

        lax.fori_loop(0, BLOCKS, mine, 0)

    def right_flow(k):
        for s in range(pairs - 1):
            @pl.when(pair == s + 1)
            def _(s=s):
                right_copy(k, s).wait_recv()

        for s in range(pairs - 1):
            @pl.when(pair == s)
            def _(s=s):
                if s > 0:
                    def body(step, carry):
                        q = step * WIDTH
                        r = (s + 1) * group + q
                        totals = weighted(raw, k, r, s)
                        if s == 1:
                            totals = plus(totals, weighted(rin, k, r, 0))
                        else:
                            totals = plus(totals, entries(rin, k, q + group))
                        for i in range(WIDTH):
                            rout[k, q + i] = totals[i]
                        return carry

                    lax.fori_loop(0, (pairs - 1 - s) * group // WIDTH, body, 0)
                right_copy(k, s).start()

    def left_flow(k):
        for s in range(1, pairs):
            @pl.when(pair == s - 1)
            def _(s=s):
                left_copy(k, s).wait_recv()

        for s in range(1, pairs):
            @pl.when(pair == s)
            def _(s=s):
                if s < pairs - 1:
                    def body(step, carry):
                        q = step * WIDTH
                        totals = weighted(raw, k, q, s)
                        if s == pairs - 2:
                            totals = plus(totals, weighted(lin, k, q, pairs - 1))
                        else:
                            totals = plus(totals, entries(lin, k, q))
                        for i in range(WIDTH):
                            lout[k, q + i] = totals[i]
                        return carry

                    lax.fori_loop(0, s * group // WIDTH, body, 0)
                left_copy(k, s).start()

    def finish(k):
        for s in range(pairs):
            @pl.when(pair == s)
            def _(s=s):
                def body(step, carry):
                    q = step * WIDTH
                    r = s * group + q
                    totals = weighted(raw, k, r, s)
                    if s == 1:
                        totals = plus(totals, weighted(rin, k, r, 0))
                    elif s > 1:
                        totals = plus(totals, entries(rin, k, q))
                    if s == pairs - 2:
                        totals = plus(totals, weighted(lin, k, r, pairs - 1))
                    elif s < pairs - 1:
                        totals = plus(totals, entries(lin, k, s * group + q))
                    for i in range(WIDTH):
                        own[k, q + i] = totals[i]
                    return carry

                lax.fori_loop(0, group // WIDTH, body, 0)

        fin_copy(k).start()
        for q in range(per_dev):
            out_ref[q, core, k] = own[k, core * per_dev + q]

    near_lag, far_lag, end_lag = 1, 2, 3
    is_left = pair < pairs // 2
    right_lag = jnp.where(is_left, near_lag, far_lag)
    left_lag = jnp.where(is_left, far_lag, near_lag)

    def step(t, carry):
        @pl.when(t < chunks)
        def _():
            produce(t)

        @pl.when((t >= 1) & (t < chunks + 1))
        def _():
            sib_wait(t - 1)

        kr = t - right_lag
        kl = t - left_lag

        @pl.when((kr >= 0) & (kr < chunks))
        def _():
            right_flow(kr)

        @pl.when((kl >= 0) & (kl < chunks))
        def _():
            left_flow(kl)

        @pl.when(t >= end_lag)
        def _():
            finish(t - end_lag)

        return carry

    lax.fori_loop(0, chunks + end_lag, step, 0)

    def drain(k, carry):
        fin_copy(k).wait_recv()
        for q in range(per_dev):
            out_ref[q, 1 - core, k] = fin[k, q]
        fin_copy(k).wait_send()
        sib_copy(k).wait_send()

        @pl.when(brick < bricks - 1)
        def _():
            up_copy(k).wait_send()

        @pl.when(brick > 0)
        def _():
            dn_copy(k).wait_send()

        for s in range(pairs - 1):
            @pl.when(pair == s)
            def _(s=s):
                right_copy(k, s).wait_send()

            @pl.when(pair == s + 1)
            def _(s=s):
                left_copy(k, s + 1).wait_send()

        return carry

    lax.fori_loop(0, chunks, drain, 0)


def sine_taper(count, extent):
    positions = jnp.arange(count, dtype=jnp.int32).astype(jnp.float32)
    return jnp.sin(jnp.pi * (positions + 0.5) / extent)


def per_device(shots, bricks, sources, slowness, group_size, window_anchor, tile_slot):
    wide_y, planes, wide_z = slowness.shape[1:]
    half_rows = wide_y // (2 * BLOCKS)
    chunks = half_rows // ROWS
    brick_index = lax.axis_index("brick")
    shot_index = lax.axis_index("shot")
    tiles = tile_slot.shape[0]
    per_dev = tiles // shots
    pairs = shots // 2
    group = 2 * per_dev
    both = 2 * BLOCKS

    extent = group_size[shot_index] * planes
    depth_ids = brick_index * planes + jnp.arange(planes, dtype=jnp.int32)
    active = depth_ids < extent
    mask = (brick_index < group_size[shot_index]).astype(jnp.float32).reshape(1)
    taper_x = jnp.where(
        active,
        jnp.sin(jnp.pi * (depth_ids.astype(jnp.float32) + 0.5) / extent.astype(jnp.float32)),
        0.0,
    )
    taper_xz = taper_x[:, None] * sine_taper(wide_z, float(wide_z))[None, :]
    taper_y = sine_taper(wide_y, float(wide_y))
    piece_slots = tile_slot[window_anchor[:, None] + jnp.arange(BLOCKS, dtype=jnp.int32)[None, :]]
    slots = jnp.arange(tiles, dtype=jnp.int32)
    weights = (slots[:, None, None] == piece_slots[None]).astype(jnp.float32).reshape(-1)

    chunk = (ROWS, planes, wide_z)
    src = sources.reshape((4, 2 * BLOCKS, chunks) + chunk)
    slow = slowness.reshape((2 * BLOCKS, chunks) + chunk)
    f32 = jnp.float32
    wide = max(both, (pairs - 2) * group)
    fwd = max(group, (pairs - 2) * group)
    dma = pltpu.SemaphoreType.DMA
    smem = pl.BlockSpec(memory_space=pltpu.SMEM)
    vmem = pl.BlockSpec(memory_space=pltpu.VMEM)
    hbm = pl.BlockSpec(memory_space=pl.ANY)
    halo = pltpu.VMEM((chunks, 4, both * ROWS, wide_z), f32)
    out = pl.pallas_call(
        functools.partial(kernel, shots, bricks, per_dev, chunks),
        out_shape=jax.ShapeDtypeStruct((per_dev, 2, chunks) + chunk, f32),
        in_specs=[smem, smem, smem, vmem, hbm, hbm],
        out_specs=vmem,
        scratch_shapes=[
            pltpu.VMEM((2, 4, both) + chunk, f32),
            pltpu.VMEM((2, both) + chunk, f32),
            pltpu.VMEM((4, wide_y + 2, planes, wide_z), f32),
            pltpu.VMEM((2, wide_y, planes, wide_z), f32),
            halo, halo, halo, halo,
            pltpu.VMEM((chunks, BLOCKS) + chunk, f32),
            pltpu.VMEM((chunks, both) + chunk, f32),
            pltpu.VMEM((chunks, wide) + chunk, f32),
            pltpu.VMEM((chunks, fwd) + chunk, f32),
            pltpu.VMEM((chunks, wide) + chunk, f32),
            pltpu.VMEM((chunks, fwd) + chunk, f32),
            pltpu.VMEM((chunks, group) + chunk, f32),
            pltpu.VMEM((chunks, per_dev) + chunk, f32),
            dma((2,)), dma((2,)),
        ] + [dma((chunks,))] * 12,
        compiler_params=pltpu.CompilerParams(
            collective_id=0, has_side_effects=True, vmem_limit_bytes=62 * 1024 * 1024
        ),
        cost_estimate=pl.CostEstimate(
            flops=200 * wide_y * planes * wide_z, bytes_accessed=12 * 1024 * 1024, transcendentals=0
        ),
    )(mask, taper_y, weights, taper_xz, src, slow)
    return out.reshape(1, per_dev, -1)


def solution(mesh):
    return jax.shard_map(
        functools.partial(per_device, mesh.shape["shot"], mesh.shape["brick"]),
        mesh=mesh,
        in_specs=(
            P("shot", None, None, None, "brick", None),
            P("shot", None, "brick", None),
            P(),
            P(),
            P(),
        ),
        out_specs=P("brick", "shot", None),
        check_vma=False,
    )
```

```python
import functools

import jax
import jax.numpy as jnp
from jax import lax
from jax.experimental import pallas as pl
from jax.experimental.pallas import tpu as pltpu
from jax.sharding import PartitionSpec as P

BLOCKS = 8
WIDTH = 2
ROWS = 4
MESH = pl.DeviceIdType.MESH

shift_beta = 0.5
relaxation = 0.8


def kernel(
    shots, bricks, per_dev, chunks,
    mask_ref, ty_ref, wt_ref, txz_ref, src_ref, slow_ref,
    out_ref,
    sbuf, wbuf, f1, inv, hs_up, hs_dn, h_before, h_after, gsend, raw,
    rin, rout, lin, lout, own, fin,
    in_sem, win_sem, up_s, up_r, dn_s, dn_r, sib_s, sib_r, rt_s, rt_r, lt_s, lt_r, fin_s, fin_r,
):
    shot = lax.axis_index("shot")
    brick = lax.axis_index("brick")
    pair, core = shot // 2, shot % 2
    sib = pair * 2 + (1 - core)
    pairs = shots // 2
    group = 2 * per_dev
    both = 2 * BLOCKS
    half_rows = chunks * ROWS
    wide_y = 2 * BLOCKS * half_rows

    def source_copies(k, slot):
        return (
            pltpu.make_async_copy(src_ref.at[:, :, k], sbuf.at[slot], in_sem.at[slot]),
            pltpu.make_async_copy(slow_ref.at[:, k], wbuf.at[slot], win_sem.at[slot]),
        )

    for copy in source_copies(0, 0):
        copy.start()

    barrier = pltpu.get_barrier_semaphore()

    def greet(s, b):
        pl.semaphore_signal(barrier, inc=1, device_id=(s, b), device_id_type=MESH)

    greet(sib, brick)

    @pl.when(brick > 0)
    def _():
        greet(shot, brick - 1)

    @pl.when(brick < bricks - 1)
    def _():
        greet(shot, brick + 1)

    @pl.when(pair > 0)
    def _():
        greet(shot - 2, brick)

    @pl.when(pair < pairs - 1)
    def _():
        greet(shot + 2, brick)

    @pl.when(brick == 0)
    def _():
        h_before[...] = jnp.zeros_like(h_before)

    @pl.when(brick == bricks - 1)
    def _():
        h_after[...] = jnp.zeros_like(h_after)

    zero_row = jnp.zeros((1,) + f1.shape[2:], jnp.float32)
    for c in range(4):
        f1[c, pl.ds(0, 1)] = zero_row
        f1[c, pl.ds(wide_y + 1, 1)] = zero_row

    one = jnp.int32(1)
    nothing = jnp.int32(0)
    friends = (
        one
        + jnp.where(brick > 0, one, nothing)
        + jnp.where(brick < bricks - 1, one, nothing)
        + jnp.where(pair > 0, one, nothing)
        + jnp.where(pair < pairs - 1, one, nothing)
    )
    pl.semaphore_wait(barrier, friends)

    def up_copy(k):
        return pltpu.make_async_remote_copy(
            src_ref=hs_up.at[k], dst_ref=h_before.at[k], send_sem=up_s.at[k], recv_sem=up_r.at[k],
            device_id=(shot, brick + 1), device_id_type=MESH)

    def dn_copy(k):
        return pltpu.make_async_remote_copy(
            src_ref=hs_dn.at[k], dst_ref=h_after.at[k], send_sem=dn_s.at[k], recv_sem=dn_r.at[k],
            device_id=(shot, brick - 1), device_id_type=MESH)

    mask = mask_ref[0]

    def first(k, carry):
        slot = lax.rem(k, 2)

        @pl.when(k + 1 < chunks)
        def _():
            for copy in source_copies(k + 1, 1 - slot):
                copy.start()

        for copy in source_copies(k, slot):
            copy.wait()

        def rows(j, carry):
            y = j * half_rows + k * ROWS
            w = wbuf[slot, j]
            real_d = 6.0 - w
            imag_d = shift_beta * w
            scale = relaxation / (real_d * real_d + imag_d * imag_d)
            ire = real_d * scale
            iim = imag_d * scale
            inv[0, pl.ds(y, ROWS)] = ire
            inv[1, pl.ds(y, ROWS)] = iim
            mre, mim = ire * mask, iim * mask
            fields = []
            for p in range(2):
                a, b = sbuf[slot, 2 * p, j], sbuf[slot, 2 * p + 1, j]
                fields += [a * mre - b * mim, a * mim + b * mre]
            for c, f in enumerate(fields):
                f1[c, pl.ds(y + 1, ROWS)] = f
                for r in range(ROWS):
                    hs_dn[k, c, pl.ds(j * ROWS + r, 1), :] = f[r, 0:1, :]
                    hs_up[k, c, pl.ds(j * ROWS + r, 1), :] = f[r, 7:8, :]
            return carry

        lax.fori_loop(0, both, rows, 0)

        @pl.when(brick < bricks - 1)
        def _():
            up_copy(k).start()

        @pl.when(brick > 0)
        def _():
            dn_copy(k).start()

        return carry

    lax.fori_loop(0, chunks, first, 0)

    planes, wide_z = f1.shape[2:]
    lane = lax.broadcasted_iota(jnp.int32, (planes, wide_z), 1)
    sub = lax.broadcasted_iota(jnp.int32, (planes, wide_z), 0)

    def image(k, j, r):
        y = j * half_rows + k * ROWS + r
        hrow = j * ROWS + r
        centre, near = [], []
        for c in range(4):
            f = f1[c, y + 1]
            total = f1[c, y] + f1[c, y + 2]
            total += jnp.where(lane == 0, 0.0, pltpu.roll(f, 1, axis=1))
            total += jnp.where(lane == wide_z - 1, 0.0, pltpu.roll(f, wide_z - 1, axis=1))
            total += jnp.where(sub == 0, h_before[k, c, pl.ds(hrow, 1), :], pltpu.roll(f, 1, axis=0))
            total += jnp.where(sub == planes - 1, h_after[k, c, pl.ds(hrow, 1), :], pltpu.roll(f, planes - 1, axis=0))
            centre.append(f)
            near.append(total)
        ire, iim = inv[0, y], inv[1, y]
        keep = 2.0 - relaxation
        field = []
        for p in (0, 2):
            field.append(keep * centre[p] + (near[p] * ire - near[p + 1] * iim))
            field.append(keep * centre[p + 1] + (near[p] * iim + near[p + 1] * ire))
        imaging = (
            field[0] * field[2]
            - field[1] * field[3]
            - shift_beta * (field[0] * field[3] + field[1] * field[2])
        )
        return imaging * (txz_ref[...] * ty_ref[y])

    def sib_copy(k):
        return pltpu.make_async_remote_copy(
            src_ref=gsend.at[k], dst_ref=raw.at[k, pl.ds(core * BLOCKS, BLOCKS)],
            send_sem=sib_s.at[k], recv_sem=sib_r.at[k],
            device_id=(sib, brick), device_id_type=MESH)

    def sib_wait(k):
        pltpu.make_async_remote_copy(
            src_ref=gsend.at[k], dst_ref=raw.at[k, pl.ds((1 - core) * BLOCKS, BLOCKS)],
            send_sem=sib_s.at[k], recv_sem=sib_r.at[k],
            device_id=(sib, brick), device_id_type=MESH).wait_recv()

    def right_copy(k, s):
        count = both if s == 0 else (pairs - 1 - s) * group
        return pltpu.make_async_remote_copy(
            src_ref=raw.at[k] if s == 0 else rout.at[k, pl.ds(0, count)],
            dst_ref=rin.at[k, pl.ds(0, count)],
            send_sem=rt_s.at[k], recv_sem=rt_r.at[k],
            device_id=(2 * (s + 1) + core, brick), device_id_type=MESH)

    def left_copy(k, s):
        count = both if s == pairs - 1 else s * group
        return pltpu.make_async_remote_copy(
            src_ref=raw.at[k] if s == pairs - 1 else lout.at[k, pl.ds(0, count)],
            dst_ref=lin.at[k, pl.ds(0, count)],
            send_sem=lt_s.at[k], recv_sem=lt_r.at[k],
            device_id=(2 * (s - 1) + core, brick), device_id_type=MESH)

    def fin_copy(k):
        return pltpu.make_async_remote_copy(
            src_ref=own.at[k, pl.ds((1 - core) * per_dev, per_dev)], dst_ref=fin.at[k],
            send_sem=fin_s.at[k], recv_sem=fin_r.at[k],
            device_id=(sib, brick), device_id_type=MESH)

    def weighted(buf, k, r, source_pair):
        starts = [((r + i) * shots + 2 * source_pair) * BLOCKS for i in range(WIDTH)]
        block = buf[k, 0]
        totals = [wt_ref[start] * block for start in starts]
        for q in range(1, both):
            block = buf[k, q]
            totals = [total + wt_ref[start + q] * block for total, start in zip(totals, starts)]
        return totals

    def plus(totals, terms):
        return [total + term for total, term in zip(totals, terms)]

    def entries(buf, k, q):
        return [buf[k, q + i] for i in range(WIDTH)]

    def produce(k):
        @pl.when(brick > 0)
        def _():
            pltpu.make_async_remote_copy(
                src_ref=hs_up.at[k], dst_ref=h_before.at[k], send_sem=up_s.at[k], recv_sem=up_r.at[k],
                device_id=(shot, brick - 1), device_id_type=MESH).wait_recv()

        @pl.when(brick < bricks - 1)
        def _():
            pltpu.make_async_remote_copy(
                src_ref=hs_dn.at[k], dst_ref=h_after.at[k], send_sem=dn_s.at[k], recv_sem=dn_r.at[k],
                device_id=(shot, brick + 1), device_id_type=MESH).wait_recv()

        def images(b, side):
            return [(b + i, r, image(k, 2 * (b + i) + side, r)) for i in range(1) for r in range(ROWS)]

        def other(step, carry):
            for b, r, value in images(step, 1 - core):
                gsend[k, b, r] = value
            return carry

        lax.fori_loop(0, BLOCKS, other, 0)
        sib_copy(k).start()

        def mine(step, carry):
            for b, r, value in images(step, core):
                raw[k, core * BLOCKS + b, r] = value
            return carry

        lax.fori_loop(0, BLOCKS, mine, 0)

    def right_flow(k):
        for s in range(pairs - 1):
            @pl.when(pair == s + 1)
            def _(s=s):
                right_copy(k, s).wait_recv()

        for s in range(pairs - 1):
            @pl.when(pair == s)
            def _(s=s):
                if s > 0:
                    def body(step, carry):
                        q = step * WIDTH
                        r = (s + 1) * group + q
                        totals = weighted(raw, k, r, s)
                        if s == 1:
                            totals = plus(totals, weighted(rin, k, r, 0))
                        else:
                            totals = plus(totals, entries(rin, k, q + group))
                        for i in range(WIDTH):
                            rout[k, q + i] = totals[i]
                        return carry

                    lax.fori_loop(0, (pairs - 1 - s) * group // WIDTH, body, 0)
                right_copy(k, s).start()

    def left_flow(k):
        for s in range(1, pairs):
            @pl.when(pair == s - 1)
            def _(s=s):
                left_copy(k, s).wait_recv()

        for s in range(1, pairs):
            @pl.when(pair == s)
            def _(s=s):
                if s < pairs - 1:
                    def body(step, carry):
                        q = step * WIDTH
                        totals = weighted(raw, k, q, s)
                        if s == pairs - 2:
                            totals = plus(totals, weighted(lin, k, q, pairs - 1))
                        else:
                            totals = plus(totals, entries(lin, k, q))
                        for i in range(WIDTH):
                            lout[k, q + i] = totals[i]
                        return carry

                    lax.fori_loop(0, s * group // WIDTH, body, 0)
                left_copy(k, s).start()

    def finish(k):
        for s in range(pairs):
            @pl.when(pair == s)
            def _(s=s):
                def body(step, carry):
                    q = step * WIDTH
                    r = s * group + q
                    totals = weighted(raw, k, r, s)
                    if s == 1:
                        totals = plus(totals, weighted(rin, k, r, 0))
                    elif s > 1:
                        totals = plus(totals, entries(rin, k, q))
                    if s == pairs - 2:
                        totals = plus(totals, weighted(lin, k, r, pairs - 1))
                    elif s < pairs - 1:
                        totals = plus(totals, entries(lin, k, s * group + q))
                    for i in range(WIDTH):
                        own[k, q + i] = totals[i]
                    return carry

                lax.fori_loop(0, group // WIDTH, body, 0)

        fin_copy(k).start()
        for q in range(per_dev):
            out_ref[q, core, k] = own[k, core * per_dev + q]

    at_end = (pair == 0) | (pair == pairs - 1)
    near_lag = jnp.where(at_end, 1, 2)
    far_lag, end_lag = 3, 4
    is_left = pair < pairs // 2
    right_lag = jnp.where(is_left, near_lag, far_lag)
    left_lag = jnp.where(is_left, far_lag, near_lag)

    def step(t, carry):
        @pl.when(t < chunks)
        def _():
            produce(t)

        @pl.when((t >= 1) & (t < chunks + 1))
        def _():
            sib_wait(t - 1)

        kr = t - right_lag
        kl = t - left_lag

        @pl.when((kr >= 0) & (kr < chunks))
        def _():
            right_flow(kr)

        @pl.when((kl >= 0) & (kl < chunks))
        def _():
            left_flow(kl)

        @pl.when(t >= end_lag)
        def _():
            finish(t - end_lag)

        return carry

    lax.fori_loop(0, chunks + end_lag, step, 0)

    def drain(k, carry):
        fin_copy(k).wait_recv()
        for q in range(per_dev):
            out_ref[q, 1 - core, k] = fin[k, q]
        fin_copy(k).wait_send()
        sib_copy(k).wait_send()

        @pl.when(brick < bricks - 1)
        def _():
            up_copy(k).wait_send()

        @pl.when(brick > 0)
        def _():
            dn_copy(k).wait_send()

        for s in range(pairs - 1):
            @pl.when(pair == s)
            def _(s=s):
                right_copy(k, s).wait_send()

            @pl.when(pair == s + 1)
            def _(s=s):
                left_copy(k, s + 1).wait_send()

        return carry

    lax.fori_loop(0, chunks, drain, 0)


def sine_taper(count, extent):
    positions = jnp.arange(count, dtype=jnp.int32).astype(jnp.float32)
    return jnp.sin(jnp.pi * (positions + 0.5) / extent)


def per_device(shots, bricks, sources, slowness, group_size, window_anchor, tile_slot):
    wide_y, planes, wide_z = slowness.shape[1:]
    half_rows = wide_y // (2 * BLOCKS)
    chunks = half_rows // ROWS
    brick_index = lax.axis_index("brick")
    shot_index = lax.axis_index("shot")
    tiles = tile_slot.shape[0]
    per_dev = tiles // shots
    pairs = shots // 2
    group = 2 * per_dev
    both = 2 * BLOCKS

    extent = group_size[shot_index] * planes
    depth_ids = brick_index * planes + jnp.arange(planes, dtype=jnp.int32)
    active = depth_ids < extent
    mask = (brick_index < group_size[shot_index]).astype(jnp.float32).reshape(1)
    taper_x = jnp.where(
        active,
        jnp.sin(jnp.pi * (depth_ids.astype(jnp.float32) + 0.5) / extent.astype(jnp.float32)),
        0.0,
    )
    taper_xz = taper_x[:, None] * sine_taper(wide_z, float(wide_z))[None, :]
    taper_y = sine_taper(wide_y, float(wide_y))
    piece_slots = tile_slot[window_anchor[:, None] + jnp.arange(BLOCKS, dtype=jnp.int32)[None, :]]
    slots = jnp.arange(tiles, dtype=jnp.int32)
    weights = (slots[:, None, None] == piece_slots[None]).astype(jnp.float32).reshape(-1)

    chunk = (ROWS, planes, wide_z)
    src = sources.reshape((4, 2 * BLOCKS, chunks) + chunk)
    slow = slowness.reshape((2 * BLOCKS, chunks) + chunk)
    f32 = jnp.float32
    wide = max(both, (pairs - 2) * group)
    fwd = max(group, (pairs - 2) * group)
    dma = pltpu.SemaphoreType.DMA
    smem = pl.BlockSpec(memory_space=pltpu.SMEM)
    vmem = pl.BlockSpec(memory_space=pltpu.VMEM)
    hbm = pl.BlockSpec(memory_space=pl.ANY)
    halo = pltpu.VMEM((chunks, 4, both * ROWS, wide_z), f32)
    out = pl.pallas_call(
        functools.partial(kernel, shots, bricks, per_dev, chunks),
        out_shape=jax.ShapeDtypeStruct((per_dev, 2, chunks) + chunk, f32),
        in_specs=[smem, smem, smem, vmem, hbm, hbm],
        out_specs=vmem,
        scratch_shapes=[
            pltpu.VMEM((2, 4, both) + chunk, f32),
            pltpu.VMEM((2, both) + chunk, f32),
            pltpu.VMEM((4, wide_y + 2, planes, wide_z), f32),
            pltpu.VMEM((2, wide_y, planes, wide_z), f32),
            halo, halo, halo, halo,
            pltpu.VMEM((chunks, BLOCKS) + chunk, f32),
            pltpu.VMEM((chunks, both) + chunk, f32),
            pltpu.VMEM((chunks, wide) + chunk, f32),
            pltpu.VMEM((chunks, fwd) + chunk, f32),
            pltpu.VMEM((chunks, wide) + chunk, f32),
            pltpu.VMEM((chunks, fwd) + chunk, f32),
            pltpu.VMEM((chunks, group) + chunk, f32),
            pltpu.VMEM((chunks, per_dev) + chunk, f32),
            dma((2,)), dma((2,)),
        ] + [dma((chunks,))] * 12,
        compiler_params=pltpu.CompilerParams(
            collective_id=0, has_side_effects=True, vmem_limit_bytes=62 * 1024 * 1024
        ),
        cost_estimate=pl.CostEstimate(
            flops=200 * wide_y * planes * wide_z, bytes_accessed=12 * 1024 * 1024, transcendentals=0
        ),
    )(mask, taper_y, weights, taper_xz, src, slow)
    return out.reshape(1, per_dev, -1)


def solution(mesh):
    return jax.shard_map(
        functools.partial(per_device, mesh.shape["shot"], mesh.shape["brick"]),
        mesh=mesh,
        in_specs=(
            P("shot", None, None, None, "brick", None),
            P("shot", None, "brick", None),
            P(),
            P(),
            P(),
        ),
        out_specs=P("brick", "shot", None),
        check_vma=False,
    )
```
